1024 devices in a mesh: row: 8 (over x), col: 128 (over y, z, core).
Axes of the slice: x: 8, y: 8, z: 8, core: 2. Of those that a mesh axis runs over, the one named last changes fastest.
Arguments:
- momentum: float32 [10240, 26624], P('row', 'col'), may hold values from -60 to 60, as said below
- grad: bfloat16 [10240, 26624], P('row', 'col'), may hold values from -6 to 6
- right_prev: float32 [26624, 128], P('col'), may hold values from -6 to 6
Outputs:
- new_momentum: float32 [10240, 26624], P('row', 'col')
- left_factor: float32 [10240, 128], P('row')
- right_next: float32 [26624, 128], P('col')
The draws below stay inside these ranges and needn't reach their ends.
Inputs may be any that keep to these rules, and one draw needn't show every extreme that they name: `momentum`: columns and rows have scales that differ.
All inputs are finite; a program needn't handle non-finite values.
Results may differ from the reference program's by a relative error of at most 0.0003.
Values sent between devices are 32-bit elements; how exact they have to be, the bound alone decides.
No kernel may reach another device: no remote copies, remote signals or barrier semaphores. Data moves between devices by JAX's collectives and lax.ppermute only.
A program may use at most 32 MiB of HBM per device.

```python
import jax
import jax.numpy as jnp
from jax import lax

D = 10240
FF = 26624
RANK = 128


def draw_momentum(key, part):
    key = jax.random.fold_in(key, 11)
    key_base, key_cols, key_rows = jax.random.split(key, 3)
    base = jnp.clip(jax.random.normal(key_base, (D, FF), jnp.float32), -4.0, 4.0)
    col_scale = jnp.exp(jax.random.uniform(key_cols, (1, FF), jnp.float32) * jnp.log(10.0)) * 0.3
    row_scale = jnp.exp(jax.random.uniform(key_rows, (D, 1), jnp.float32) * jnp.log(3.0)) * 0.6
    return base * col_scale * row_scale


def level_of(own_key, dims, cuts, least, top_value):
    def one(position, parts):
        draws = jax.random.uniform(jax.random.fold_in(jax.random.fold_in(own_key, 6), position), (parts,), jnp.float32, least / len(cuts), top_value / len(cuts))
        return jnp.repeat(jnp.exp(draws), dims[position] // parts).reshape((-1,) + (1,) * (len(dims) - position - 1))

    factor_of = one(*cuts[0])
    for cut in cuts[1:]:
        factor_of = factor_of * one(*cut)
    return factor_of


def normal_values(key, dims, scale, reach, pieces=(), held_as=jnp.bfloat16):
    drawn = jax.random.normal(key, dims, jnp.float32) * scale
    if len(pieces) > 0:
        drawn = level_of(key, dims, pieces, -0.22, 0.18) * drawn
    return jnp.clip(drawn, min=-reach, max=reach).astype(held_as)


def setup_inputs(seed: int = 0) -> dict:
    key_of = jax.random.split(jax.random.key(seed), 4)
    momentum = draw_momentum(jax.random.fold_in(key_of[3], 71), 0)
    grad = normal_values(key_of[1], (D, FF), 1.0, 6.0, ((0, 8), (1, 128)))
    right_prev = normal_values(key_of[2], (FF, RANK), 1.0, 6.0, ((0, 128),), jnp.float32)
    return {"momentum": momentum, "grad": grad, "right_prev": right_prev}


feedback = 0.05
eps = 1e-06
high = lax.Precision.HIGHEST

def reference(momentum, grad, right_prev):
    buffer = momentum + grad.astype(jnp.float32)
    proj = jnp.dot(buffer.astype(jnp.float32), right_prev.astype(jnp.float32), precision=high, preferred_element_type=jnp.float32)
    gram = jnp.dot(proj.T.astype(jnp.float32), proj.astype(jnp.float32), precision=high, preferred_element_type=jnp.float32)
    lower = jnp.linalg.cholesky(gram)
    basis = lax.linalg.triangular_solve(lower, proj, left_side=False, lower=True, transpose_a=True)
    back = lax.dot_general(buffer.astype(jnp.float32), basis.astype(jnp.float32), (((0,), (0,)), ((), ())), precision=high, preferred_element_type=jnp.float32)
    squares = lax.optimization_barrier(jnp.sum(back * back, axis=0))
    right_next = back * lax.rsqrt(squares / FF + eps)
    new_momentum = buffer - feedback * jnp.dot(basis.astype(jnp.float32), back.T.astype(jnp.float32), precision=high, preferred_element_type=jnp.float32)
    left_factor = basis * jnp.sqrt(jnp.float32(D))
    return (new_momentum, left_factor, right_next)
```

```python
import jax
import jax.numpy as jnp
from jax import lax
from jax.sharding import Mesh, PartitionSpec as P

D = 10240
FF = 26624
RANK = 128

feedback = 0.05
eps = 1e-06
high = lax.Precision.HIGHEST
col = ("y", "z", "core")


def mm(a, b, dims):
    return lax.dot_general(a, b, (dims, ((), ())), precision=high, preferred_element_type=jnp.float32)


def exchange(parts, axis):
    return lax.all_to_all(parts, axis, 0, 0)


def copies(x, n):
    return jnp.broadcast_to(x[None], (n,) + x.shape)


def sum_over_col(partial):
    rows = partial.shape[0]
    half = jnp.sum(exchange(partial.reshape(2, rows // 2, RANK), "core"), axis=0)
    share = jnp.sum(exchange(half.reshape(8, rows // 16, RANK), "y"), axis=0)
    share = jnp.sum(exchange(copies(share, 8), "z"), axis=0)
    half = exchange(copies(share, 8), "y").reshape(rows // 2, RANK)
    return lax.all_gather(half, "core", axis=0, tiled=True)


def sum_over_row(partial):
    rows, width = partial.shape
    share = jnp.sum(exchange(partial.reshape(8, rows // 8, width), "row"), axis=0)
    return exchange(copies(share, 8), "row").reshape(rows, width)


def sum_small(x):
    x = lax.psum(x, "core")
    x = jnp.sum(exchange(copies(x, 8), "y"), axis=0)
    return jnp.sum(exchange(copies(x, 8), "z"), axis=0)


def per_device(momentum, grad, right_prev):
    buffer = momentum + grad.astype(jnp.float32)
    proj = sum_over_col(mm(buffer, right_prev, ((1,), (0,))))
    products = jnp.concatenate(
        [mm(proj, proj, ((0,), (0,))), mm(proj, buffer, ((0,), (0,)))], axis=1
    )
    products = sum_over_row(products)
    gram, raw = products[:, :RANK], products[:, RANK:]
    lower = jnp.linalg.cholesky(gram)
    inverse = lax.linalg.triangular_solve(
        lower, jnp.eye(RANK, dtype=jnp.float32), left_side=True, lower=True
    )
    back = mm(raw, inverse, ((0,), (1,)))
    basis = mm(proj, inverse, ((1,), (1,)))
    squares = sum_small(jnp.sum((back * back).reshape(-1, 8, RANK), axis=0))
    squares = jnp.sum(squares, axis=0, keepdims=True)
    right_next = back * lax.rsqrt(squares / FF + eps)
    new_momentum = buffer - feedback * mm(basis, back, ((1,), (1,)))
    left_factor = basis * jnp.sqrt(jnp.float32(D))
    return (new_momentum, left_factor, right_next)


def solution(mesh):
    fine = Mesh(mesh.devices.reshape(8, 8, 8, 2), ("row", "y", "z", "core"))
    return jax.shard_map(
        per_device,
        mesh=fine,
        in_specs=(P("row", col), P("row", col), P(col, None)),
        out_specs=(P("row", col), P("row", None), P(col, None)),
        check_vma=False,
    )
```

```python
import jax
import jax.numpy as jnp
from jax import lax
from jax.experimental import pallas as pl
from jax.experimental.pallas import tpu as pltpu
from jax.sharding import Mesh, PartitionSpec as P

D = 10240
FF = 26624
RANK = 128

feedback = 0.05
eps = 1e-06
high = lax.Precision.HIGHEST
col = ("y", "z", "core")


def mm(a, b, dims):
    return lax.dot_general(a, b, (dims, ((), ())), precision=high, preferred_element_type=jnp.float32)


def exchange(parts, axis):
    return lax.all_to_all(parts, axis, 0, 0)


def copies(x, n):
    return jnp.broadcast_to(x[None], (n,) + x.shape)


def sum_over_col(partial):
    rows = partial.shape[0]
    half = jnp.sum(exchange(partial.reshape(2, rows // 2, RANK), "core"), axis=0)
    share = jnp.sum(exchange(half.reshape(8, rows // 16, RANK), "y"), axis=0)
    share = jnp.sum(exchange(copies(share, 8), "z"), axis=0)
    half = exchange(copies(share, 8), "y").reshape(rows // 2, RANK)
    return lax.all_gather(half, "core", axis=0, tiled=True)


def sum_over_row(partial):
    rows, width = partial.shape
    share = jnp.sum(exchange(partial.reshape(8, rows // 8, width), "row"), axis=0)
    return exchange(copies(share, 8), "row").reshape(rows, width)


def sum_small(x):
    x = lax.psum(x, "core")
    x = jnp.sum(exchange(copies(x, 8), "y"), axis=0)
    return jnp.sum(exchange(copies(x, 8), "z"), axis=0)


def factor_inverse(gram_ref, out_ref):
    tile = (8, RANK)
    lane = lax.broadcasted_iota(jnp.int32, tile, 1)
    sub = lax.broadcasted_iota(jnp.int32, tile, 0)
    rows = [gram_ref[8 * t : 8 * t + 8, :] for t in range(RANK // 8)]
    for k in range(RANK // 8):
        first = 8 * k
        panel = rows[k]
        inside = (lane >= first) & (lane < first + 8)
        cols = [jnp.broadcast_to(panel[:, first + q : first + q + 1], tile) for q in range(8)]
        a = {}
        for q in range(8):
            for p in range(q + 1):
                a[p, q] = jnp.broadcast_to(cols[q][p : p + 1, :], tile)
        inv, m = [], {}
        for p in range(8):
            inv.append(1.0 / a[p, p])
            for q in range(p + 1, 8):
                m[q, p] = a[p, q] * inv[p]
            for q in range(p + 1, 8):
                for s in range(q, 8):
                    a[q, s] = a[q, s] - m[q, p] * a[p, s]
        start = jnp.where(inside, (lane - first == sub).astype(jnp.float32), panel)
        r = []
        for i in range(8):
            row = jnp.broadcast_to(start[i : i + 1, :], tile)
            for p in range(i):
                row = row - m[i, p] * r[p]
            r.append(row)
        done = jnp.zeros(tile, jnp.float32)
        for i in range(8):
            done = jnp.where(sub == i, r[i] * lax.rsqrt(a[i, i]), done)
        out_ref[first : first + 8, :] = jnp.where(lane <= first + sub, done, 0.0)
        for t in range(k + 1, RANK // 8):
            c = [jnp.broadcast_to(rows[t][:, first + q : first + q + 1], tile) for q in range(8)]
            row = jnp.where(inside, 0.0, rows[t])
            for p in range(8):
                w = c[p] * inv[p]
                for q in range(p + 1, 8):
                    c[q] = c[q] - w * a[p, q]
                row = row - w * r[p]
            rows[t] = row


def inverse_factor(gram):
    return pl.pallas_call(
        factor_inverse,
        out_shape=jax.ShapeDtypeStruct((RANK, RANK), jnp.float32),
        in_specs=[pl.BlockSpec(memory_space=pltpu.VMEM)],
        out_specs=pl.BlockSpec(memory_space=pltpu.VMEM),
    )(gram)


def per_device(momentum, grad, right_prev):
    buffer = momentum + grad.astype(jnp.float32)
    proj = sum_over_col(mm(buffer, right_prev, ((1,), (0,))))
    products = jnp.concatenate(
        [mm(proj, proj, ((0,), (0,))), mm(proj, buffer, ((0,), (0,)))], axis=1
    )
    products = sum_over_row(products)
    gram, raw = products[:, :RANK], products[:, RANK:]
    inverse = inverse_factor(gram)
    back = mm(raw, inverse, ((0,), (1,)))
    basis = mm(proj, inverse, ((1,), (1,)))
    squares = sum_small(jnp.sum((back * back).reshape(-1, 8, RANK), axis=0))
    squares = jnp.sum(squares, axis=0, keepdims=True)
    right_next = back * lax.rsqrt(squares / FF + eps)
    new_momentum = buffer - feedback * mm(basis, back, ((1,), (1,)))
    left_factor = basis * jnp.sqrt(jnp.float32(D))
    return (new_momentum, left_factor, right_next)


def solution(mesh):
    fine = Mesh(mesh.devices.reshape(8, 8, 8, 2), ("row", "y", "z", "core"))
    return jax.shard_map(
        per_device,
        mesh=fine,
        in_specs=(P("row", col), P("row", col), P(col, None)),
        out_specs=(P("row", col), P("row", None), P(col, None)),
        check_vma=False,
    )
```

```python
import jax
import jax.numpy as jnp
from jax import lax
from jax.experimental import pallas as pl
from jax.experimental.pallas import tpu as pltpu
from jax.sharding import Mesh, PartitionSpec as P

D = 10240
FF = 26624
RANK = 128

feedback = 0.05
eps = 1e-06
high = lax.Precision.HIGHEST
col = ("y", "z", "core")


def mm(a, b, dims):
    return lax.dot_general(a, b, (dims, ((), ())), precision=high, preferred_element_type=jnp.float32)


def exchange(parts, axis):
    return lax.all_to_all(parts, axis, 0, 0)


def copies(x, n):
    return jnp.broadcast_to(x[None], (n,) + x.shape)


def sum_over_col(partial):
    rows = partial.shape[0]
    half = jnp.sum(exchange(partial.reshape(2, rows // 2, RANK), "core"), axis=0)
    share = jnp.sum(exchange(half.reshape(8, rows // 16, RANK), "y"), axis=0)
    share = jnp.sum(exchange(copies(share, 8), "z"), axis=0)
    half = exchange(copies(share, 8), "y").reshape(rows // 2, RANK)
    return lax.all_gather(half, "core", axis=0, tiled=True)


def sum_over_row(partial):
    rows, width = partial.shape
    share = jnp.sum(exchange(partial.reshape(8, rows // 8, width), "row"), axis=0)
    return exchange(copies(share, 8), "row").reshape(rows, width)


def factor_inverse(products_ref, inverse_ref):
    tile = (8, RANK)
    lane = lax.broadcasted_iota(jnp.int32, tile, 1)
    sub = lax.broadcasted_iota(jnp.int32, tile, 0)
    rows = [products_ref[8 * t : 8 * t + 8, :RANK] for t in range(RANK // 8)]
    for k in range(RANK // 8):
        first = 8 * k
        panel = rows[k]
        inside = (lane >= first) & (lane < first + 8)
        cols = [jnp.broadcast_to(panel[:, first + q : first + q + 1], tile) for q in range(8)]
        a = {}
        for q in range(8):
            for p in range(q + 1):
                a[p, q] = jnp.broadcast_to(cols[q][p : p + 1, :], tile)
        inv, m = [], {}
        for p in range(8):
            inv.append(1.0 / a[p, p])
            for q in range(p + 1, 8):
                m[q, p] = a[p, q] * inv[p]
            for q in range(p + 1, 8):
                for s in range(q, 8):
                    a[q, s] = a[q, s] - m[q, p] * a[p, s]
        start = jnp.where(inside, (lane - first == sub).astype(jnp.float32), panel)
        r = []
        for i in range(8):
            row = jnp.broadcast_to(start[i : i + 1, :], tile)
            for p in range(i):
                row = row - m[i, p] * r[p]
            r.append(row)
        done = jnp.zeros(tile, jnp.float32)
        for i in range(8):
            done = jnp.where(sub == i, r[i] * lax.rsqrt(a[i, i]), done)
        inverse_ref[first : first + 8, :] = jnp.where(lane <= first + sub, done, 0.0)
        for t in range(k + 1, RANK // 8):
            c = [jnp.broadcast_to(rows[t][:, first + q : first + q + 1], tile) for q in range(8)]
            row = jnp.where(inside, 0.0, rows[t])
            for p in range(8):
                w = c[p] * inv[p]
                for q in range(p + 1, 8):
                    c[q] = c[q] - w * a[p, q]
                row = row - w * r[p]
            rows[t] = row


def back_kernel(products_ref, inverse_ref, back_ref, squares_ref):
    factor_inverse(products_ref, inverse_ref)
    back = mm(products_ref[:, RANK:].T, inverse_ref[...], ((1,), (1,)))
    back_ref[...] = back
    squares = jnp.sum((back * back).reshape(-1, 8, RANK), axis=0)
    for i in range(squares_ref.shape[0]):
        squares_ref[i] = squares


def proj_kernel(momentum_ref, grad_ref, right_ref, out_ref):
    for i in range(out_ref.shape[0] // 256):
        part = slice(256 * i, 256 * i + 256)
        buffer = momentum_ref[:, part] + grad_ref[:, part].astype(jnp.float32)
        out_ref[part, :] = mm(buffer, right_ref[...], ((0,), (0,)))


def per_device(momentum, grad, right_prev):
    rows, width = momentum.shape
    partial = pl.pallas_call(
        proj_kernel, out_shape=jax.ShapeDtypeStruct((rows, RANK), jnp.float32)
    )(momentum.T, grad.T, right_prev)
    proj = sum_over_col(partial)
    buffer = momentum + grad.astype(jnp.float32)
    products = jnp.concatenate(
        [mm(proj, proj, ((0,), (0,))), mm(proj, buffer, ((0,), (0,)))], axis=1
    )
    products = sum_over_row(products)
    inverse, back, squares = pl.pallas_call(
        back_kernel,
        out_shape=(
            jax.ShapeDtypeStruct((RANK, RANK), jnp.float32),
            jax.ShapeDtypeStruct((width, RANK), jnp.float32),
            jax.ShapeDtypeStruct((16, 8, RANK), jnp.float32),
        ),
    )(products)
    basis = mm(proj, inverse, ((1,), (1,)))
    squares = jnp.sum(exchange(squares, ("y", "core")), axis=0)
    squares = jnp.sum(exchange(copies(squares, 8), "z"), axis=(0, 1))
    right_next = back * lax.rsqrt(squares / FF + eps)
    new_momentum = buffer - feedback * mm(basis, back, ((1,), (1,)))
    left_factor = basis * jnp.sqrt(jnp.float32(D))
    return (new_momentum, left_factor, right_next)


def solution(mesh):
    fine = Mesh(mesh.devices.reshape(8, 8, 8, 2), ("row", "y", "z", "core"))
    return jax.shard_map(
        per_device,
        mesh=fine,
        in_specs=(P("row", col), P("row", col), P(col, None)),
        out_specs=(P("row", col), P("row", None), P(col, None)),
        check_vma=False,
    )
```

```python
import jax
import jax.numpy as jnp
from jax import lax
from jax.experimental import pallas as pl
from jax.experimental.pallas import tpu as pltpu
from jax.sharding import Mesh, PartitionSpec as P

D = 10240
FF = 26624
RANK = 128

feedback = 0.05
eps = 1e-06
high = lax.Precision.HIGHEST
col = ("y", "z", "core")


def mm(a, b, dims):
    return lax.dot_general(a, b, (dims, ((), ())), precision=high, preferred_element_type=jnp.float32)


def exchange(parts, axis):
    return lax.all_to_all(parts, axis, 0, 0)


def copies(x, n):
    return jnp.broadcast_to(x[None], (n,) + x.shape)


def sum_over_col(partial):
    rows = partial.shape[0]
    half = jnp.sum(exchange(partial.reshape(2, rows // 2, RANK), "core"), axis=0)
    share = jnp.sum(exchange(half.reshape(8, rows // 16, RANK), "y"), axis=0)
    share = jnp.sum(exchange(copies(share, 8), "z"), axis=0)
    half = exchange(copies(share, 8), "y").reshape(rows // 2, RANK)
    return lax.all_gather(half, "core", axis=0, tiled=True)


def sum_over_row(partial):
    rows, width = partial.shape
    share = jnp.sum(exchange(partial.reshape(8, rows // 8, width), "row"), axis=0)
    return exchange(copies(share, 8), "row").reshape(rows, width)


def factor_inverse(products_ref, inverse_ref):
    tile = (8, RANK)
    lane = lax.broadcasted_iota(jnp.int32, tile, 1)
    sub = lax.broadcasted_iota(jnp.int32, tile, 0)
    rows = [products_ref[8 * t : 8 * t + 8, :RANK] for t in range(RANK // 8)]
    for k in range(RANK // 8):
        first = 8 * k
        panel = rows[k]
        inside = (lane >= first) & (lane < first + 8)
        cols = [jnp.broadcast_to(panel[:, first + q : first + q + 1], tile) for q in range(8)]
        a = {}
        for q in range(8):
            for p in range(q + 1):
                a[p, q] = jnp.broadcast_to(cols[q][p : p + 1, :], tile)
        inv, m = [], {}
        for p in range(8):
            inv.append(1.0 / a[p, p])
            for q in range(p + 1, 8):
                m[q, p] = a[p, q] * inv[p]
            for q in range(p + 1, 8):
                for s in range(q, 8):
                    a[q, s] = a[q, s] - m[q, p] * a[p, s]
        start = jnp.where(inside, (lane - first == sub).astype(jnp.float32), panel)
        r = []
        for i in range(8):
            row = jnp.broadcast_to(start[i : i + 1, :], tile)
            for p in range(i):
                row = row - m[i, p] * r[p]
            r.append(row)
        done = jnp.zeros(tile, jnp.float32)
        for i in range(8):
            done = jnp.where(sub == i, r[i] * lax.rsqrt(a[i, i]), done)
        inverse_ref[first : first + 8, :] = jnp.where(lane <= first + sub, done, 0.0)
        for t in range(k + 1, RANK // 8):
            c = [jnp.broadcast_to(rows[t][:, first + q : first + q + 1], tile) for q in range(8)]
            row = jnp.where(inside, 0.0, rows[t])
            for p in range(8):
                w = c[p] * inv[p]
                for q in range(p + 1, 8):
                    c[q] = c[q] - w * a[p, q]
                row = row - w * r[p]
            rows[t] = row


def back_kernel(products_ref, inverse_ref, back_ref, squares_ref):
    factor_inverse(products_ref, inverse_ref)
    back = mm(products_ref[:, RANK:].T, inverse_ref[...], ((1,), (1,)))
    back_ref[...] = back
    squares = jnp.sum((back * back).reshape(-1, 8, RANK), axis=0)
    for i in range(squares_ref.shape[0]):
        squares_ref[i] = squares


def proj_kernel(momentum_ref, grad_ref, right_ref, out_ref):
    for i in range(out_ref.shape[0] // 256):
        part = slice(256 * i, 256 * i + 256)
        buffer = momentum_ref[:, part] + grad_ref[:, part].astype(jnp.float32)
        out_ref[part, :] = mm(buffer, right_ref[...], ((0,), (0,)))


def per_device(momentum, grad, right_prev):
    rows, width = momentum.shape
    partial = pl.pallas_call(
        proj_kernel, out_shape=pltpu.VMEM((rows, RANK), jnp.float32)
    )(momentum.T, grad.T, right_prev)
    proj = sum_over_col(partial)
    buffer = momentum + grad.astype(jnp.float32)
    products = jnp.concatenate(
        [mm(proj, proj, ((0,), (0,))), mm(proj, buffer, ((0,), (0,)))], axis=1
    )
    products = sum_over_row(products)
    inverse, back, squares = pl.pallas_call(
        back_kernel,
        out_shape=(
            pltpu.VMEM((RANK, RANK), jnp.float32),
            pltpu.VMEM((width, RANK), jnp.float32),
            jax.ShapeDtypeStruct((16, 8, RANK), jnp.float32),
        ),
    )(pltpu.with_memory_space_constraint(products, pltpu.VMEM))
    basis = mm(proj, inverse, ((1,), (1,)))
    squares = jnp.sum(exchange(squares, ("y", "core")), axis=0)
    new_momentum = buffer - feedback * mm(basis, back, ((1,), (1,)))
    squares, new_momentum = lax.optimization_barrier((squares, new_momentum))
    squares = jnp.sum(exchange(copies(squares, 8), "z"), axis=(0, 1))
    right_next = back * lax.rsqrt(squares / FF + eps)
    left_factor = basis * jnp.sqrt(jnp.float32(D))
    return (new_momentum, left_factor, right_next)


def solution(mesh):
    fine = Mesh(mesh.devices.reshape(8, 8, 8, 2), ("row", "y", "z", "core"))
    return jax.shard_map(
        per_device,
        mesh=fine,
        in_specs=(P("row", col), P("row", col), P(col, None)),
        out_specs=(P("row", col), P("row", None), P(col, None)),
        check_vma=False,
    )
```

```python
import jax
import jax.numpy as jnp
from jax import lax
from jax.experimental import pallas as pl
from jax.experimental.pallas import tpu as pltpu
from jax.sharding import Mesh, PartitionSpec as P

D = 10240
FF = 26624
RANK = 128

feedback = 0.05
eps = 1e-06
high = lax.Precision.HIGHEST
col = ("y", "z", "core")


def mm(a, b, dims):
    return lax.dot_general(a, b, (dims, ((), ())), precision=high, preferred_element_type=jnp.float32)


def lines(first, second):
    along = {
        "y": lambda core: [[(y * 8 + z) * 2 + core for y in range(8)] for z in range(8)],
        "z": lambda core: [[(y * 8 + z) * 2 + core for z in range(8)] for y in range(8)],
    }
    return along[first](0) + along[second](1)


def exchange(parts, axis, groups=None):
    return lax.all_to_all(parts, axis, 0, 0, axis_index_groups=groups)


def copies(x, n):
    return jnp.broadcast_to(x[None], (n,) + x.shape)


def sum_over_col(partial):
    rows = partial.shape[0]
    half = jnp.sum(exchange(partial.reshape(2, rows // 2, RANK), "core"), axis=0)
    one, other = lines("y", "z"), lines("z", "y")
    share = jnp.sum(exchange(half.reshape(8, rows // 16, RANK), col, one), axis=0)
    share = jnp.sum(exchange(copies(share, 8), col, other), axis=0)
    half = exchange(copies(share, 8), col, one).reshape(rows // 2, RANK)
    return lax.all_gather(half, "core", axis=0, tiled=True)


def sum_over_row(partial):
    rows, width = partial.shape
    share = jnp.sum(exchange(partial.reshape(8, rows // 8, width), "row"), axis=0)
    return exchange(copies(share, 8), "row").reshape(rows, width)


def factor_inverse(products_ref, inverse_ref):
    tile = (8, RANK)
    lane = lax.broadcasted_iota(jnp.int32, tile, 1)
    sub = lax.broadcasted_iota(jnp.int32, tile, 0)
    rows = [products_ref[8 * t : 8 * t + 8, :RANK] for t in range(RANK // 8)]
    for k in range(RANK // 8):
        first = 8 * k
        panel = rows[k]
        inside = (lane >= first) & (lane < first + 8)
        cols = [jnp.broadcast_to(panel[:, first + q : first + q + 1], tile) for q in range(8)]
        a = {}
        for q in range(8):
            for p in range(q + 1):
                a[p, q] = jnp.broadcast_to(cols[q][p : p + 1, :], tile)
        inv, m = [], {}
        for p in range(8):
            inv.append(1.0 / a[p, p])
            for q in range(p + 1, 8):
                m[q, p] = a[p, q] * inv[p]
            for q in range(p + 1, 8):
                for s in range(q, 8):
                    a[q, s] = a[q, s] - m[q, p] * a[p, s]
        start = jnp.where(inside, (lane - first == sub).astype(jnp.float32), panel)
        r = []
        for i in range(8):
            row = jnp.broadcast_to(start[i : i + 1, :], tile)
            for p in range(i):
                row = row - m[i, p] * r[p]
            r.append(row)
        done = jnp.zeros(tile, jnp.float32)
        for i in range(8):
            done = jnp.where(sub == i, r[i] * lax.rsqrt(a[i, i]), done)
        inverse_ref[first : first + 8, :] = jnp.where(lane <= first + sub, done, 0.0)
        for t in range(k + 1, RANK // 8):
            c = [jnp.broadcast_to(rows[t][:, first + q : first + q + 1], tile) for q in range(8)]
            row = jnp.where(inside, 0.0, rows[t])
            for p in range(8):
                w = c[p] * inv[p]
                for q in range(p + 1, 8):
                    c[q] = c[q] - w * a[p, q]
                row = row - w * r[p]
            rows[t] = row


def back_kernel(products_ref, inverse_ref, back_ref, squares_ref):
    factor_inverse(products_ref, inverse_ref)
    back = mm(products_ref[:, RANK:].T, inverse_ref[...], ((1,), (1,)))
    back_ref[...] = back
    squares = jnp.sum(back * back, axis=0, keepdims=True)
    for i in range(squares_ref.shape[0]):
        squares_ref[i] = squares


def proj_kernel(momentum_ref, grad_ref, right_ref, out_ref):
    for i in range(out_ref.shape[0] // 256):
        part = slice(256 * i, 256 * i + 256)
        buffer = momentum_ref[:, part] + grad_ref[:, part].astype(jnp.float32)
        out_ref[part, :] = mm(buffer, right_ref[...], ((0,), (0,)))


def per_device(momentum, grad, right_prev):
    rows, width = momentum.shape
    partial = pl.pallas_call(
        proj_kernel, out_shape=pltpu.VMEM((rows, RANK), jnp.float32)
    )(momentum.T, grad.T, right_prev)
    proj = sum_over_col(partial)
    buffer = momentum + grad.astype(jnp.float32)
    products = jnp.concatenate(
        [mm(proj, proj, ((0,), (0,))), mm(proj, buffer, ((0,), (0,)))], axis=1
    )
    products = sum_over_row(products)
    inverse, back, squares = pl.pallas_call(
        back_kernel,
        out_shape=(
            pltpu.VMEM((RANK, RANK), jnp.float32),
            pltpu.VMEM((width, RANK), jnp.float32),
            jax.ShapeDtypeStruct((16, 1, RANK), jnp.float32),
        ),
    )(pltpu.with_memory_space_constraint(products, pltpu.VMEM))
    basis = mm(proj, inverse, ((1,), (1,)))
    squares = jnp.sum(exchange(squares, ("y", "core")), axis=0)
    new_momentum = buffer - feedback * mm(basis, back, ((1,), (1,)))
    squares, new_momentum = lax.optimization_barrier((squares, new_momentum))
    squares = jnp.sum(exchange(copies(squares, 8), "z"), axis=(0, 1))
    right_next = back * lax.rsqrt(squares / FF + eps)
    left_factor = basis * jnp.sqrt(jnp.float32(D))
    return (new_momentum, left_factor, right_next)


def solution(mesh):
    fine = Mesh(mesh.devices.reshape(8, 8, 8, 2), ("row", "y", "z", "core"))
    return jax.shard_map(
        per_device,
        mesh=fine,
        in_specs=(P("row", col), P("row", col), P(col, None)),
        out_specs=(P("row", col), P("row", None), P(col, None)),
        check_vma=False,
    )
```

```python
import jax
import jax.numpy as jnp
from jax import lax
from jax.experimental import pallas as pl
from jax.experimental.pallas import tpu as pltpu
from jax.sharding import Mesh, PartitionSpec as P

D = 10240
FF = 26624
RANK = 128

feedback = 0.05
eps = 1e-06
high = lax.Precision.HIGHEST
col = ("y", "z", "core")


def mm(a, b, dims):
    return lax.dot_general(a, b, (dims, ((), ())), precision=high, preferred_element_type=jnp.float32)


def lines(first, second):
    along = {
        "y": lambda core: [[(y * 8 + z) * 2 + core for y in range(8)] for z in range(8)],
        "z": lambda core: [[(y * 8 + z) * 2 + core for z in range(8)] for y in range(8)],
    }
    return along[first](0) + along[second](1)


def exchange(parts, axis, groups=None):
    return lax.all_to_all(parts, axis, 0, 0, axis_index_groups=groups)


def copies(x, n):
    return jnp.broadcast_to(x[None], (n,) + x.shape)


def sum_over_col(partial):
    rows = partial.shape[0]
    half = jnp.sum(exchange(partial.reshape(2, rows // 2, RANK), "core"), axis=0)
    one, other = lines("y", "z"), lines("z", "y")
    share = jnp.sum(exchange(half.reshape(8, rows // 16, RANK), col, one), axis=0)
    share = jnp.sum(exchange(copies(share, 8), col, other), axis=0)
    half = exchange(copies(share, 8), col, one).reshape(rows // 2, RANK)
    return lax.all_gather(half, "core", axis=0, tiled=True)


def sum_over_row(partial):
    rows, width = partial.shape
    share = jnp.sum(exchange(partial.reshape(8, rows // 8, width), "row"), axis=0)
    return exchange(copies(share, 8), "row").reshape(rows, width)


def factor_inverse(products_ref, inverse_ref):
    tile = (8, RANK)
    lane = lax.broadcasted_iota(jnp.int32, tile, 1)
    sub = lax.broadcasted_iota(jnp.int32, tile, 0)
    rows = [products_ref[8 * t : 8 * t + 8, :RANK] for t in range(RANK // 8)]
    for k in range(RANK // 8):
        first = 8 * k
        panel = rows[k]
        inside = (lane >= first) & (lane < first + 8)
        cols = [jnp.broadcast_to(panel[:, first + q : first + q + 1], tile) for q in range(8)]
        a = {}
        for q in range(8):
            for p in range(q + 1):
                a[p, q] = jnp.broadcast_to(cols[q][p : p + 1, :], tile)
        inv, m = [], {}
        for p in range(8):
            inv.append(1.0 / a[p, p])
            for q in range(p + 1, 8):
                m[q, p] = a[p, q] * inv[p]
            for q in range(p + 1, 8):
                for s in range(q, 8):
                    a[q, s] = a[q, s] - m[q, p] * a[p, s]
        start = jnp.where(inside, (lane - first == sub).astype(jnp.float32), panel)
        r = []
        for i in range(8):
            row = jnp.broadcast_to(start[i : i + 1, :], tile)
            for p in range(i):
                row = row - m[i, p] * r[p]
            r.append(row)
        done = jnp.zeros(tile, jnp.float32)
        for i in range(8):
            done = jnp.where(sub == i, r[i] * lax.rsqrt(a[i, i]), done)
        inverse_ref[first : first + 8, :] = jnp.where(lane <= first + sub, done, 0.0)
        for t in range(k + 1, RANK // 8):
            c = [jnp.broadcast_to(rows[t][:, first + q : first + q + 1], tile) for q in range(8)]
            row = jnp.where(inside, 0.0, rows[t])
            for p in range(8):
                w = c[p] * inv[p]
                for q in range(p + 1, 8):
                    c[q] = c[q] - w * a[p, q]
                row = row - w * r[p]
            rows[t] = row


def back_kernel(products_ref, inverse_ref, back_ref, squares_ref):
    factor_inverse(products_ref, inverse_ref)
    back = mm(products_ref[:, RANK:].T, inverse_ref[...], ((1,), (1,)))
    back_ref[...] = back
    squares = jnp.sum(back * back, axis=0, keepdims=True)
    for i in range(squares_ref.shape[0]):
        squares_ref[i] = squares


def proj_kernel(momentum_ref, grad_ref, right_ref, out_ref):
    for i in range(out_ref.shape[0] // 256):
        part = slice(256 * i, 256 * i + 256)
        buffer = momentum_ref[:, part] + grad_ref[:, part].astype(jnp.float32)
        out_ref[part, :] = mm(buffer, right_ref[...], ((0,), (0,)))


def products_kernel(proj_ref, momentum_ref, grad_ref, out_ref):
    proj = proj_ref[...]
    buffer = momentum_ref[...] + grad_ref[...].astype(jnp.float32)
    out_ref[:, :RANK] = mm(proj, proj, ((0,), (0,)))
    out_ref[:, RANK:] = mm(buffer, proj, ((1,), (0,))).T


def outputs_kernel(proj_ref, inverse_ref, back_ref, momentum_ref, grad_ref, left_ref, feedback_ref):
    basis = mm(proj_ref[...], inverse_ref[...], ((1,), (1,)))
    left_ref[...] = basis * D**0.5
    buffer = momentum_ref[...] + grad_ref[...].astype(jnp.float32)
    feedback_ref[...] = buffer - feedback * mm(back_ref[...], basis, ((1,), (1,)))


def in_vmem(x):
    return pltpu.with_memory_space_constraint(x, pltpu.VMEM)


def per_device(momentum, grad, right_prev):
    rows, width = momentum.shape
    partial = pl.pallas_call(
        proj_kernel, out_shape=pltpu.VMEM((rows, RANK), jnp.float32)
    )(momentum.T, grad.T, right_prev)
    proj = sum_over_col(partial)
    momentum_t, grad_t, proj = in_vmem(momentum.T), in_vmem(grad.T), in_vmem(proj)
    products = pl.pallas_call(
        products_kernel, out_shape=pltpu.VMEM((RANK, RANK + width), jnp.float32)
    )(proj, momentum_t, grad_t)
    products = sum_over_row(products)
    inverse, back, squares = pl.pallas_call(
        back_kernel,
        out_shape=(
            pltpu.VMEM((RANK, RANK), jnp.float32),
            pltpu.VMEM((width, RANK), jnp.float32),
            jax.ShapeDtypeStruct((128, 1, RANK), jnp.float32),
        ),
    )(in_vmem(products))
    squares = jnp.sum(exchange(squares, col), axis=(0, 1))
    left_factor, new_momentum = pl.pallas_call(
        outputs_kernel,
        out_shape=(
            jax.ShapeDtypeStruct((rows, RANK), jnp.float32),
            jax.ShapeDtypeStruct((width, rows), jnp.float32),
        ),
        cost_estimate=pl.CostEstimate(
            flops=12 * rows * RANK * (RANK + width),
            bytes_accessed=4 * rows * (RANK + 2 * width),
            transcendentals=0,
        ),
    )(proj, in_vmem(inverse), in_vmem(back), momentum_t, grad_t)
    right_next = back * lax.rsqrt(squares / FF + eps)
    return (new_momentum.T, left_factor, right_next)


def solution(mesh):
    fine = Mesh(mesh.devices.reshape(8, 8, 8, 2), ("row", "y", "z", "core"))
    return jax.shard_map(
        per_device,
        mesh=fine,
        in_specs=(P("row", col), P("row", col), P(col, None)),
        out_specs=(P("row", col), P("row", None), P(col, None)),
        check_vma=False,
    )
```

```python
import jax
import jax.numpy as jnp
from jax import lax
from jax.experimental import pallas as pl
from jax.experimental.pallas import tpu as pltpu
from jax.sharding import Mesh, PartitionSpec as P

D = 10240
FF = 26624
RANK = 128

feedback = 0.05
eps = 1e-06
high = lax.Precision.HIGHEST
col = ("y", "z", "core")


def mm(a, b, dims):
    return lax.dot_general(a, b, (dims, ((), ())), precision=high, preferred_element_type=jnp.float32)


def lines(first, second):
    along = {
        "y": lambda core: [[(y * 8 + z) * 2 + core for y in range(8)] for z in range(8)],
        "z": lambda core: [[(y * 8 + z) * 2 + core for z in range(8)] for y in range(8)],
    }
    return along[first](0) + along[second](1)


def exchange(parts, axis, groups=None):
    return lax.all_to_all(parts, axis, 0, 0, axis_index_groups=groups)


def copies(x, n):
    return jnp.broadcast_to(x[None], (n,) + x.shape)


def sum_over_col(away, own):
    rows = 2 * own.shape[0]
    half = own + lax.ppermute(away, "core", [(0, 1), (1, 0)])
    one, other = lines("y", "z"), lines("z", "y")
    share = jnp.sum(exchange(half.reshape(8, rows // 16, RANK), col, one), axis=0)
    share = jnp.sum(exchange(copies(share, 8), col, other), axis=0)
    half = exchange(copies(share, 8), col, one).reshape(rows // 2, RANK)
    return lax.all_gather(half, "core", axis=0, tiled=True)


def sum_over_row(partial):
    rows, width = partial.shape
    share = jnp.sum(exchange(partial.reshape(8, rows // 8, width), "row"), axis=0)
    return exchange(copies(share, 8), "row").reshape(rows, width)


def factor_inverse(products_ref, inverse_ref):
    tile = (8, RANK)
    lane = lax.broadcasted_iota(jnp.int32, tile, 1)
    sub = lax.broadcasted_iota(jnp.int32, tile, 0)
    rows = [products_ref[8 * t : 8 * t + 8, :RANK] for t in range(RANK // 8)]
    for k in range(RANK // 8):
        first = 8 * k
        panel = rows[k]
        inside = (lane >= first) & (lane < first + 8)
        cols = [jnp.broadcast_to(panel[:, first + q : first + q + 1], tile) for q in range(8)]
        a = {}
        for q in range(8):
            for p in range(q + 1):
                a[p, q] = jnp.broadcast_to(cols[q][p : p + 1, :], tile)
        inv, m = [], {}
        for p in range(8):
            inv.append(1.0 / a[p, p])
            for q in range(p + 1, 8):
                m[q, p] = a[p, q] * inv[p]
            for q in range(p + 1, 8):
                for s in range(q, 8):
                    a[q, s] = a[q, s] - m[q, p] * a[p, s]
        start = jnp.where(inside, (lane - first == sub).astype(jnp.float32), panel)
        r = []
        for i in range(8):
            row = jnp.broadcast_to(start[i : i + 1, :], tile)
            for p in range(i):
                row = row - m[i, p] * r[p]
            r.append(row)
        done = jnp.zeros(tile, jnp.float32)
        for i in range(8):
            done = jnp.where(sub == i, r[i] * lax.rsqrt(a[i, i]), done)
        inverse_ref[first : first + 8, :] = jnp.where(lane <= first + sub, done, 0.0)
        for t in range(k + 1, RANK // 8):
            c = [jnp.broadcast_to(rows[t][:, first + q : first + q + 1], tile) for q in range(8)]
            row = jnp.where(inside, 0.0, rows[t])
            for p in range(8):
                w = c[p] * inv[p]
                for q in range(p + 1, 8):
                    c[q] = c[q] - w * a[p, q]
                row = row - w * r[p]
            rows[t] = row


def back_kernel(products_ref, inverse_ref, back_ref, squares_ref):
    factor_inverse(products_ref, inverse_ref)
    back = mm(products_ref[:, RANK:].T, inverse_ref[...], ((1,), (1,)))
    back_ref[...] = back
    squares = jnp.sum(back * back, axis=0, keepdims=True)
    for i in range(squares_ref.shape[0]):
        squares_ref[i] = squares


def proj_kernel(core_ref, momentum_ref, grad_ref, right_ref, away_ref, own_ref):
    rows = own_ref.shape[0]
    for ref, side in ((away_ref, 1 - core_ref[0]), (own_ref, core_ref[0])):
        part = pl.ds(pl.multiple_of(side * rows, rows), rows)
        buffer = momentum_ref[:, part] + grad_ref[:, part].astype(jnp.float32)
        ref[...] = mm(buffer, right_ref[...], ((0,), (0,)))


def products_kernel(proj_ref, momentum_ref, grad_ref, out_ref):
    proj = proj_ref[...]
    buffer = momentum_ref[...] + grad_ref[...].astype(jnp.float32)
    out_ref[:, :RANK] = mm(proj, proj, ((0,), (0,)))
    out_ref[:, RANK:] = mm(buffer, proj, ((1,), (0,))).T


def outputs_kernel(proj_ref, inverse_ref, back_ref, momentum_ref, grad_ref, left_ref, feedback_ref):
    basis = mm(proj_ref[...], inverse_ref[...], ((1,), (1,)))
    left_ref[...] = basis * D**0.5
    buffer = momentum_ref[...] + grad_ref[...].astype(jnp.float32)
    feedback_ref[...] = buffer - feedback * mm(back_ref[...], basis, ((1,), (1,)))


def in_vmem(x):
    return pltpu.with_memory_space_constraint(x, pltpu.VMEM)


def per_device(momentum, grad, right_prev):
    rows, width = momentum.shape
    vmem = pl.BlockSpec(memory_space=pltpu.VMEM)
    away, own = pl.pallas_call(
        proj_kernel,
        out_shape=(pltpu.VMEM((rows // 2, RANK), jnp.float32),) * 2,
        in_specs=[pl.BlockSpec(memory_space=pltpu.SMEM), vmem, vmem, vmem],
    )(lax.axis_index("core").reshape(1), momentum.T, grad.T, right_prev)
    proj = sum_over_col(away, own)
    momentum_t, grad_t, proj = in_vmem(momentum.T), in_vmem(grad.T), in_vmem(proj)
    products = pl.pallas_call(
        products_kernel, out_shape=pltpu.VMEM((RANK, RANK + width), jnp.float32)
    )(proj, momentum_t, grad_t)
    products = sum_over_row(products)
    inverse, back, squares = pl.pallas_call(
        back_kernel,
        out_shape=(
            pltpu.VMEM((RANK, RANK), jnp.float32),
            pltpu.VMEM((width, RANK), jnp.float32),
            pltpu.VMEM((128, 1, RANK), jnp.float32),
        ),
    )(in_vmem(products))
    squares = jnp.sum(exchange(squares, col), axis=(0, 1))
    left_factor, new_momentum = pl.pallas_call(
        outputs_kernel,
        out_shape=(
            jax.ShapeDtypeStruct((rows, RANK), jnp.float32),
            jax.ShapeDtypeStruct((width, rows), jnp.float32),
        ),
        cost_estimate=pl.CostEstimate(
            flops=12 * rows * RANK * (RANK + width),
            bytes_accessed=4 * rows * (RANK + 2 * width),
            transcendentals=0,
        ),
    )(proj, in_vmem(inverse), in_vmem(back), momentum_t, grad_t)
    right_next = back * lax.rsqrt(squares / FF + eps)
    return (new_momentum.T, left_factor, right_next)


def solution(mesh):
    fine = Mesh(mesh.devices.reshape(8, 8, 8, 2), ("row", "y", "z", "core"))
    return jax.shard_map(
        per_device,
        mesh=fine,
        in_specs=(P("row", col), P("row", col), P(col, None)),
        out_specs=(P("row", col), P("row", None), P(col, None)),
        check_vma=False,
    )
```
